256 devices in a mesh: blk: 32 (over z, x_lo, core), quarter: 8 (over y, x_hi).
Axes of the slice: x: 4 (x_hi: 2, x_lo: 2; x = x_hi * 2 + x_lo), y: 4, z: 8, core: 2. Of those that a mesh axis runs over, the one named last changes fastest.
Arguments:
- sensor: bfloat16 [8192, 1024], P(('blk', 'quarter')), may hold values from -24 to 24
- video: bfloat16 [8192, 1024], P(('blk', 'quarter')), may hold values from -24 to 24
- sens_ref: bfloat16 [1024, 1024], replicated, may hold values from -0.25 to 0.25
- vid_ref: bfloat16 [1024, 1024], replicated, may hold values from -0.25 to 0.25
- sens_val: bfloat16 [1024, 1024], replicated, may hold values from -0.1875 to 0.1875
- vid_val: bfloat16 [1024, 1024], replicated, may hold values from -0.1875 to 0.1875
- sens_out: bfloat16 [1024, 1024], replicated, may hold values from -0.1875 to 0.1875
- vid_out: bfloat16 [1024, 1024], replicated, may hold values from -0.1875 to 0.1875
- sens_gain: float32 [1024], replicated, may hold values from 0.5 to 1.5
- vid_gain: float32 [1024], replicated, may hold values from 0.5 to 1.5
Outputs:
- sensor_next: bfloat16 [8192, 1024], P(('blk', 'quarter'))
- video_next: bfloat16 [8192, 1024], P(('blk', 'quarter'))
The draws below stay inside these ranges and needn't reach their ends.
All inputs are finite; a program needn't handle non-finite values.
Results may differ from the reference program's by a relative error of at most 0.0099.
Values may be sent and summed in bfloat16 or wider, within the bound.
A program may use at most 64 MiB of HBM per device.

```python
import math
import jax
import jax.numpy as jnp
from jax import lax

D = 1024
H = 16
TOKENS = 8192


def drawn_stream(key, salt):
    own = jax.random.fold_in(key, salt)
    base = jnp.clip(jax.random.normal(own, (TOKENS, D), jnp.float32), -6.0, 6.0)
    return base.astype(jnp.bfloat16)


def draw_sensor(key, part):
    return drawn_stream(key, 11)


def draw_video(key, part):
    return drawn_stream(key, 12)


def shrink_along(matrix, key):
    return matrix


def reference_pair(key):
    first = jnp.clip(jax.random.normal(jax.random.fold_in(key, 41), (D, D), jnp.float32), -3.9, 3.9)
    second = jnp.clip(jax.random.normal(jax.random.fold_in(key, 42), (D, D), jnp.float32), -3.9, 3.9)
    return (first, second)


def draw_sens_ref(key, part):
    first, second = reference_pair(key)
    matrix = shrink_along(2.0 * first / jnp.sqrt(jnp.float32(D)), key)
    return jnp.clip(matrix, -0.25, 0.25).astype(jnp.bfloat16)


def draw_vid_ref(key, part):
    first, second = reference_pair(key)
    matrix = shrink_along(2.0 * (0.9 * first + 0.44 * second) / jnp.sqrt(jnp.float32(D)), key)
    return jnp.clip(matrix, -0.25, 0.25).astype(jnp.bfloat16)


def noise(own_key, dims, deviation, most, kind=jnp.bfloat16):
    result = jax.random.normal(own_key, dims, jnp.float32) * deviation
    return jnp.minimum(jnp.maximum(result, -most), most).astype(kind)


def setup_inputs(seed: int = 0) -> dict:
    streams_of = jax.random.split(jax.random.key(seed), 11)
    sensor = draw_sensor(jax.random.fold_in(streams_of[10], 71), 0)
    video = draw_video(jax.random.fold_in(streams_of[10], 71), 0)
    sens_ref = draw_sens_ref(jax.random.fold_in(streams_of[10], 71), 0)
    vid_ref = draw_vid_ref(jax.random.fold_in(streams_of[10], 71), 0)
    sens_val = noise(streams_of[4], (D, D), D ** -0.5, 0.1875)
    vid_val = noise(streams_of[5], (D, D), D ** -0.5, 0.1875)
    sens_out = noise(streams_of[6], (D, D), D ** -0.5, 0.1875)
    vid_out = noise(streams_of[7], (D, D), D ** -0.5, 0.1875)
    sens_gain = jnp.clip(1.0 + 0.1 * jax.random.normal(streams_of[8], (D,), jnp.float32), 0.5, 1.5)
    vid_gain = jnp.clip(1.0 + 0.1 * jax.random.normal(streams_of[9], (D,), jnp.float32), 0.5, 1.5)
    return {"sensor": sensor, "video": video, "sens_ref": sens_ref, "vid_ref": vid_ref, "sens_val": sens_val, "vid_val": vid_val, "sens_out": sens_out, "vid_out": vid_out, "sens_gain": sens_gain, "vid_gain": vid_gain}


def project(inputs, weight):
    return jnp.dot(inputs, weight, preferred_element_type=jnp.float32).astype(jnp.bfloat16)

def heads_first(matrix):
    return matrix.reshape(matrix.shape[0], H, D // H).transpose(1, 0, 2)

def attend(query_ref, key_ref, values):
    block_rows = math.gcd(query_ref.shape[0], 2048)
    blocks = query_ref.reshape(-1, block_rows, query_ref.shape[1])
    score_scale = (D // H) ** (-0.5)

    def one_block(query_rows):
        scores = jnp.dot(query_rows, key_ref.T, preferred_element_type=jnp.float32) * score_scale
        highest = lax.optimization_barrier(jnp.max(scores, axis=1, keepdims=True))
        weights = jnp.exp(scores - highest)
        totals = lax.optimization_barrier(jnp.sum(weights, axis=1, keepdims=True))
        mixed = jnp.dot(weights.astype(jnp.bfloat16), values, preferred_element_type=jnp.float32)
        return mixed / totals
    return lax.map(one_block, blocks).reshape(query_ref.shape[0], -1)

def head_pair(pieces):
    sens_r, sens_u, vid_r, vid_u = pieces
    return (attend(sens_r, vid_r, vid_u), attend(vid_r, sens_r, sens_u))

def finish(inputs, mixed, gain, weight):
    power = lax.optimization_barrier(jnp.mean(mixed * mixed, axis=-1, keepdims=True))
    normed = (mixed * lax.rsqrt(power + 1e-06) * gain).astype(jnp.bfloat16)
    update = jnp.dot(normed, weight, preferred_element_type=jnp.float32)
    return (inputs.astype(jnp.float32) + update).astype(jnp.bfloat16)

def reference(sensor, video, sens_ref, vid_ref, sens_val, vid_val, sens_out, vid_out, sens_gain, vid_gain):
    sens_r = project(sensor, sens_ref)
    sens_u = project(sensor, sens_val)
    vid_r = project(video, vid_ref)
    vid_u = project(video, vid_val)
    sens_heads, vid_heads = lax.map(head_pair, (heads_first(sens_r), heads_first(sens_u), heads_first(vid_r), heads_first(vid_u)))
    sens_attn = sens_heads.transpose(1, 0, 2).reshape(TOKENS, D)
    vid_attn = vid_heads.transpose(1, 0, 2).reshape(TOKENS, D)
    return (finish(sensor, sens_attn, sens_gain, sens_out), finish(video, vid_attn, vid_gain, vid_out))
```

```python
import functools
import math

import jax
import jax.numpy as jnp
from jax import lax
from jax.experimental import pallas as pl
from jax.experimental.pallas import tpu as pltpu
from jax.sharding import PartitionSpec as P

H = 16
MESH = pl.DeviceIdType.MESH
F32 = jnp.float32
BF16 = jnp.bfloat16
NX = 4
NY = 4
NP = 16
ROWS = 32
D = 1024
LANES = 128
HEAD = 64
CHUNK = NP * ROWS
TOK = NX * CHUNK
NT = (((1,), (1,)), ((), ()))
C2 = math.log2(math.e) * HEAD ** -0.5
AUG = 80
BLK = 256


def kernel(
    sensor, video, w_sr, w_vr, w_su, w_vu, w_so, w_vo, s_gain, v_gain,
    s_next, v_next,
    wbuf, stage, sb, vb, s_ut, v_ut, num_out, st_out, num_in, st_in, a_out, a_in, sbuf,
    w_sem, z_send, z_recv, g_send, g_recv, n_send, n_recv, t_send, t_recv, r_send, r_recv,
):
    blk = lax.axis_index("blk")
    quarter = lax.axis_index("quarter")
    core = blk % 2
    x_lo = (blk // 2) % 2
    z = blk // 4
    x_hi = quarter % 2
    y = quarter // 2
    x = x_hi * 2 + x_lo
    p = z * 2 + core

    def zc_peer(q):
        return (((q // 2) * 2 + x_lo) * 2 + q % 2, quarter)

    def x_peer(k):
        return ((z * 2 + k % 2) * 2 + core, y * 2 + k // 2)

    def y_peer(k):
        return (blk, k * 2 + x_hi)

    weights = (w_sr, w_su, w_vr, w_vu, w_so, w_vo)
    loads = [pltpu.make_async_copy(w, wbuf.at[k], w_sem.at[k]) for k, w in enumerate(weights)]
    for load in loads:
        load.start()

    barrier = pltpu.get_barrier_semaphore()

    def greet_zc(d, _):
        pl.semaphore_signal(barrier, inc=1, device_id=zc_peer((p + d) % NP), device_id_type=MESH)
        return 0

    def greet_xy(d, _):
        pl.semaphore_signal(barrier, inc=1, device_id=x_peer((x + d) % NX), device_id_type=MESH)
        pl.semaphore_signal(barrier, inc=1, device_id=y_peer((y + d) % NY), device_id_type=MESH)
        return 0

    lax.fori_loop(1, NP, greet_zc, 0)
    lax.fori_loop(1, NX, greet_xy, 0)

    low = lax.broadcasted_iota(jnp.int32, (ROWS, LANES), 1) < HEAD

    def project(rows, first, slot):
        loads[first].wait()
        ref = jnp.dot(rows[...], wbuf[first], preferred_element_type=F32)
        loads[first + 1].wait()
        val = jnp.dot(rows[...], wbuf[first + 1], preferred_element_type=F32)
        for k in range(H // 2):
            a = ref[:, k * LANES:(k + 1) * LANES]
            b = val[:, k * LANES:(k + 1) * LANES]
            stage[slot, 2 * k] = jnp.where(low, a, pltpu.roll(b, HEAD, 1)).astype(BF16)
            stage[slot, 2 * k + 1] = jnp.where(low, pltpu.roll(a, HEAD, 1), b).astype(BF16)

    def send_heads(slot, dst, own):
        def send(d, _):
            q = (p + d) % NP
            pltpu.make_async_remote_copy(
                src_ref=stage.at[slot, q], dst_ref=dst.at[own, p],
                send_sem=z_send.at[slot, q], recv_sem=z_recv.at[slot, p],
                device_id=zc_peer(q), device_id_type=MESH,
            ).start()
            return 0

        lax.fori_loop(1, NP, send, 0)
        dst[own, p] = stage[slot, p]

    def await_heads(slot, dst, own):
        def wait(d, _):
            q = (p + d) % NP
            pltpu.make_async_remote_copy(
                src_ref=stage.at[slot, q], dst_ref=dst.at[own, q],
                send_sem=z_send.at[slot, q], recv_sem=z_recv.at[slot, q],
                device_id=zc_peer(q), device_id_type=MESH,
            ).wait()
            return 0

        lax.fori_loop(1, NP, wait, 0)

    project(sensor, 0, 0)
    pl.semaphore_wait(barrier, (NP - 1) + (NX - 1) + (NY - 1))
    send_heads(0, sb, x)
    project(video, 2, 1)
    send_heads(1, vb, y)

    def gather(slot, buf, own, peer, k):
        return pltpu.make_async_remote_copy(
            src_ref=buf.at[own], dst_ref=buf.at[own],
            send_sem=g_send.at[slot, k], recv_sem=g_recv.at[slot, own],
            device_id=peer(k), device_id_type=MESH,
        )

    def gathered(slot, buf, own, peer, k):
        return pltpu.make_async_remote_copy(
            src_ref=buf.at[own], dst_ref=buf.at[k],
            send_sem=g_send.at[slot, k], recv_sem=g_recv.at[slot, k],
            device_id=peer(k), device_id_type=MESH,
        )

    await_heads(0, sb, x)
    for d in (2, 1, 3):
        gather(0, sb, x, x_peer, (x + d) % NX).start()
    await_heads(1, vb, y)
    for d in (2, 1, 3):
        gather(1, vb, y, y_peer, (y + d) % NY).start()
    for d in (1, 3, 2):
        gathered(0, sb, x, x_peer, (x + d) % NX).wait()
    for d in (1, 3, 2):
        gathered(1, vb, y, y_peer, (y + d) % NY).wait()

    pick = (
        lax.broadcasted_iota(jnp.int32, (AUG, LANES), 1)
        == lax.broadcasted_iota(jnp.int32, (AUG, LANES), 0) + (LANES - AUG)
    )
    ones_row = lax.broadcasted_iota(jnp.int32, (AUG, LANES), 0) < AUG - HEAD
    select = jnp.where(jnp.logical_and(pick, jnp.logical_not(ones_row)), 1.0, 0.0).astype(BF16)

    def transposed(src, dst):
        def part(k, _):
            t = lax.dot_general(
                select, src[k].reshape(CHUNK, LANES), NT, preferred_element_type=F32
            )
            head = lax.broadcasted_iota(jnp.int32, (AUG, CHUNK), 0) < AUG - HEAD
            dst[k] = jnp.where(head, 1.0, t).astype(BF16)
            return 0

        lax.fori_loop(0, NX, part, 0)

    transposed(sb, s_ut)
    transposed(vb, v_ut)

    keep = lax.broadcasted_iota(jnp.int32, (CHUNK, LANES), 1) < HEAD

    def attend(slot, own_side, other_side, other_ut, own, peer):
        def one(d, _):
            k = (own + d) % NX
            mine = jnp.where(
                keep, own_side[k].reshape(CHUNK, LANES), jnp.zeros((), BF16)
            )
            for half in range(CHUNK // BLK):
                cols = slice(half * BLK, (half + 1) * BLK)
                query = mine[cols]
                tops = []
                for j in range(NX):
                    s = lax.dot_general(
                        other_side[j].reshape(CHUNK, LANES), query, NT,
                        preferred_element_type=F32,
                    )
                    sbuf[j] = s
                    tops.append(jnp.max(s, axis=0, keepdims=True))
                top = jnp.maximum(jnp.maximum(tops[0], tops[1]), jnp.maximum(tops[2], tops[3]))
                acc = jnp.zeros((AUG, BLK), F32)
                for j in range(NX):
                    w = jnp.exp2((sbuf[j] - top) * C2).astype(BF16)
                    acc = acc + jnp.dot(other_ut[j], w, preferred_element_type=F32)
                num_out[slot, k, :, cols] = acc[AUG - HEAD:].astype(BF16)
                st_out[slot, k, 0:8, cols] = acc[0:8]
                st_out[slot, k, 8:16, cols] = jnp.broadcast_to(top, (8, BLK))

            @pl.when(d < NX)
            def _():
                pltpu.make_async_remote_copy(
                    src_ref=num_out.at[slot, k], dst_ref=num_in.at[slot, own],
                    send_sem=n_send.at[slot, k], recv_sem=n_recv.at[slot, own],
                    device_id=peer(k), device_id_type=MESH,
                ).start()
                pltpu.make_async_remote_copy(
                    src_ref=st_out.at[slot, k], dst_ref=st_in.at[slot, own],
                    send_sem=t_send.at[slot, k], recv_sem=t_recv.at[slot, own],
                    device_id=peer(k), device_id_type=MESH,
                ).start()

            return 0

        lax.fori_loop(1, NX + 1, one, 0)

    def combine(slot, own, peer):
        for d in (1, 2, 3):
            k = (own + d) % NX
            pltpu.make_async_remote_copy(
                src_ref=num_out.at[slot, k], dst_ref=num_in.at[slot, k],
                send_sem=n_send.at[slot, k], recv_sem=n_recv.at[slot, k],
                device_id=peer(k), device_id_type=MESH,
            ).wait()
            pltpu.make_async_remote_copy(
                src_ref=st_out.at[slot, k], dst_ref=st_in.at[slot, k],
                send_sem=t_send.at[slot, k], recv_sem=t_recv.at[slot, k],
                device_id=peer(k), device_id_type=MESH,
            ).wait()
        num_in[slot, own] = num_out[slot, own]
        st_in[slot, own] = st_out[slot, own]
        tops = [st_in[slot, k, 8:9, :] for k in range(NX)]
        top = jnp.maximum(jnp.maximum(tops[0], tops[1]), jnp.maximum(tops[2], tops[3]))
        total = jnp.zeros((1, CHUNK), F32)
        mixed = jnp.zeros((HEAD, CHUNK), F32)
        for k in range(NX):
            fade = jnp.exp2((tops[k] - top) * C2)
            total = total + st_in[slot, k, 0:1, :] * fade
            mixed = mixed + num_in[slot, k].astype(F32) * fade
        return mixed / total

    attend(0, sb, vb, v_ut, x, x_peer)
    attend(1, vb, sb, s_ut, y, y_peer)
    sens_attn = combine(0, x, x_peer)
    vid_attn = combine(1, y, y_peer)
    both = jnp.concatenate([sens_attn, vid_attn], axis=0)
    a_out[...] = both.T.astype(BF16).reshape(NP, ROWS, LANES)

    def send_back(d, _):
        q = (p + d) % NP
        pltpu.make_async_remote_copy(
            src_ref=a_out.at[q], dst_ref=a_in.at[p],
            send_sem=r_send.at[q], recv_sem=r_recv.at[p],
            device_id=zc_peer(q), device_id_type=MESH,
        ).start()
        return 0

    lax.fori_loop(1, NP, send_back, 0)
    a_in[p] = a_out[p]

    def wait_back(d, _):
        q = (p + d) % NP
        pltpu.make_async_remote_copy(
            src_ref=a_out.at[q], dst_ref=a_in.at[q],
            send_sem=r_send.at[q], recv_sem=r_recv.at[q],
            device_id=zc_peer(q), device_id_type=MESH,
        ).wait()
        return 0

    lax.fori_loop(1, NP, wait_back, 0)

    sens_parts, vid_parts = [], []
    for k in range(H // 2):
        a = a_in[2 * k].astype(F32)
        b = a_in[2 * k + 1].astype(F32)
        sens_parts.append(jnp.where(low, a, pltpu.roll(b, HEAD, 1)))
        vid_parts.append(jnp.where(low, pltpu.roll(a, HEAD, 1), b))

    def finish(rows, parts, gain, slot, out):
        loads[slot].wait()
        mixed = jnp.concatenate(parts, axis=1)
        power = jnp.mean(mixed * mixed, axis=-1, keepdims=True)
        normed = (mixed * lax.rsqrt(power + 1e-6) * gain[...]).astype(BF16)
        update = jnp.dot(normed, wbuf[slot], preferred_element_type=F32)
        out[...] = (rows[...].astype(F32) + update).astype(BF16)

    finish(sensor, sens_parts, s_gain, 4, s_next)
    finish(video, vid_parts, v_gain, 5, v_next)


def local(sensor, video, w_sr, w_vr, w_su, w_vu, w_so, w_vo, s_gain, v_gain):
    vmem = pl.BlockSpec(memory_space=pltpu.VMEM)
    hbm = pl.BlockSpec(memory_space=pl.ANY)
    dma = pltpu.SemaphoreType.DMA
    return pl.pallas_call(
        kernel,
        out_shape=(
            jax.ShapeDtypeStruct(sensor.shape, sensor.dtype),
            jax.ShapeDtypeStruct(video.shape, video.dtype),
        ),
        in_specs=[vmem, vmem] + [hbm] * 6 + [vmem, vmem],
        out_specs=(vmem, vmem),
        scratch_shapes=[
            pltpu.VMEM((6, D, D), BF16),
            pltpu.VMEM((2, NP, ROWS, LANES), BF16),
            pltpu.VMEM((NX, NP, ROWS, LANES), BF16),
            pltpu.VMEM((NY, NP, ROWS, LANES), BF16),
            pltpu.VMEM((NX, AUG, CHUNK), BF16),
            pltpu.VMEM((NY, AUG, CHUNK), BF16),
            pltpu.VMEM((2, NX, HEAD, CHUNK), BF16),
            pltpu.VMEM((2, NX, 16, CHUNK), F32),
            pltpu.VMEM((2, NX, HEAD, CHUNK), BF16),
            pltpu.VMEM((2, NX, 16, CHUNK), F32),
            pltpu.VMEM((NP, ROWS, LANES), BF16),
            pltpu.VMEM((NP, ROWS, LANES), BF16),
            pltpu.VMEM((NX, CHUNK, BLK), F32),
            dma((6,)),
            dma((2, NP)), dma((2, NP)),
            dma((2, NX)), dma((2, NX)),
            dma((2, NX)), dma((2, NX)),
            dma((2, NX)), dma((2, NX)),
            dma((NP,)), dma((NP,)),
        ],
        compiler_params=pltpu.CompilerParams(
            collective_id=0, has_side_effects=True, vmem_limit_bytes=56 * 1024 * 1024
        ),
    )(
        sensor, video, w_sr, w_vr, w_su, w_vu, w_so, w_vo,
        s_gain.reshape(1, D), v_gain.reshape(1, D),
    )


def solution(mesh):
    rows = P(("blk", "quarter"), None)
    return jax.shard_map(
        local,
        mesh=mesh,
        in_specs=(rows, rows) + (P(),) * 8,
        out_specs=(rows, rows),
        check_vma=False,
    )
```

```python
import functools
import math

import jax
import jax.numpy as jnp
from jax import lax
from jax.experimental import pallas as pl
from jax.experimental.pallas import tpu as pltpu
from jax.sharding import PartitionSpec as P

H = 16
MESH = pl.DeviceIdType.MESH
F32 = jnp.float32
BF16 = jnp.bfloat16
NX = 4
NY = 4
NP = 16
ROWS = 32
D = 1024
LANES = 128
HEAD = 64
CHUNK = NP * ROWS
TOK = NX * CHUNK
NT = (((1,), (1,)), ((), ()))
C2 = math.log2(math.e) * HEAD ** -0.5
AUG = 80
BLK = 256
HALF = NP // 2


def shift_z(t):
    return (t % 2) * ((t + 1) // 2) - (1 - t % 2) * (t // 2)


def shift_xy(o):
    return o + o // 2 - 2 * (o // 3)


MIRROR = (0, 2, 1, 3)


def kernel(
    sensor, video, w_sr, w_vr, w_su, w_vu, w_so, w_vo, s_gain, v_gain,
    update_out,
    wbuf, stage, chunks, uts, num_out, st_out, num_in, st_in, a_out, a_in, queries, accs, tops, sbuf_a, sbuf_b,
    w_sem, z_send, z_recv, g_send, g_recv, n_send, n_recv, t_send, t_recv, r_send, r_recv,
):
    blk = lax.axis_index("blk")
    quarter = lax.axis_index("quarter")
    core = blk % 2
    x_lo = (blk // 2) % 2
    z = blk // 4
    x_hi = quarter % 2
    y = quarter // 2
    x = x_hi * 2 + x_lo
    p = z * 2 + core

    def zc_peer(q):
        return (((q // 2) * 2 + x_lo) * 2 + q % 2, quarter)

    def x_peer(d):
        k = (x + d) % NX
        return ((z * 2 + k % 2) * 2 + core, y * 2 + k // 2)

    def y_peer(d):
        return (blk, (y + d) % NY * 2 + x_hi)

    peers = (x_peer, y_peer)
    weights = (w_sr, w_su, w_vr, w_vu, w_so, w_vo)
    loads = [pltpu.make_async_copy(w, wbuf.at[k], w_sem.at[k]) for k, w in enumerate(weights)]
    for load in loads:
        load.start()

    barrier = pltpu.get_barrier_semaphore()

    def greet_zc(d, _):
        pl.semaphore_signal(barrier, inc=1, device_id=zc_peer((p + d) % NP), device_id_type=MESH)
        return 0

    def greet_xy(d, _):
        pl.semaphore_signal(barrier, inc=1, device_id=x_peer(d), device_id_type=MESH)
        pl.semaphore_signal(barrier, inc=1, device_id=y_peer(d), device_id_type=MESH)
        return 0

    lax.fori_loop(1, NP, greet_zc, 0)
    lax.fori_loop(1, NX, greet_xy, 0)

    low = lax.broadcasted_iota(jnp.int32, (ROWS, LANES), 1) < HEAD

    def project(rows, first, side):
        loads[first].wait()
        ref = jnp.dot(rows[...], wbuf[first], preferred_element_type=F32)
        loads[first + 1].wait()
        val = jnp.dot(rows[...], wbuf[first + 1], preferred_element_type=F32)
        for k in range(H // 2):
            a = ref[:, k * LANES:(k + 1) * LANES]
            b = val[:, k * LANES:(k + 1) * LANES]
            stage[side, 2 * k] = jnp.where(low, a, pltpu.roll(b, HEAD, 1)).astype(BF16)
            stage[side, 2 * k + 1] = jnp.where(low, pltpu.roll(a, HEAD, 1), b).astype(BF16)

    def head_copy(side, s, sender):
        t = s // 2
        sign = -1 if sender else 1
        q = (z + sign * shift_z(t) + HALF) % HALF * 2 + s % 2
        return pltpu.make_async_remote_copy(
            src_ref=stage.at[side, q],
            dst_ref=chunks.at[side, 0, t * 2 + core if sender else s],
            send_sem=z_send.at[side, s],
            recv_sem=z_recv.at[side, t * 2 + core if sender else s],
            device_id=zc_peer(q), device_id_type=MESH,
        )

    def send_heads(side):
        def send(i, _):
            head_copy(side, (core + 15 - i) % NP, True).start()
            return 0

        lax.fori_loop(0, NP - 1, send, 0)
        chunks[side, 0, core] = stage[side, p]

    def await_heads(side, group):
        def wait(d, _):
            s = (core + d) % HALF if group == 0 else HALF + d
            head_copy(side, s, False).wait()
            return 0

        lax.fori_loop(1 if group == 0 else 0, HALF, wait, 0)

    def gather_copy(side, group, o):
        part = pl.ds(group * HALF, HALF)
        return pltpu.make_async_remote_copy(
            src_ref=chunks.at[side, 0, part], dst_ref=chunks.at[side, MIRROR[o], part],
            send_sem=g_send.at[side, group, o], recv_sem=g_recv.at[side, group, MIRROR[o]],
            device_id=peers[side](shift_xy(o)), device_id_type=MESH,
        )

    def gathered(side, group, o):
        part = pl.ds(group * HALF, HALF)
        return pltpu.make_async_remote_copy(
            src_ref=chunks.at[side, 0, part], dst_ref=chunks.at[side, o, part],
            send_sem=g_send.at[side, group, o], recv_sem=g_recv.at[side, group, o],
            device_id=peers[side](shift_xy(o)), device_id_type=MESH,
        )

    project(sensor, 0, 0)
    pl.semaphore_wait(barrier, (NP - 1) + (NX - 1) + (NY - 1))
    send_heads(0)
    project(video, 2, 1)
    send_heads(1)
    for group in range(2):
        for side in range(2):
            await_heads(side, group)
            for o in (1, 2):
                gather_copy(side, group, o).start()
    for group in range(2):
        for side in range(2):
            gather_copy(side, group, 3).start()

    head_rows = lax.broadcasted_iota(jnp.int32, (AUG, LANES), 0) < AUG - HEAD
    pick = (
        lax.broadcasted_iota(jnp.int32, (AUG, LANES), 1)
        == lax.broadcasted_iota(jnp.int32, (AUG, LANES), 0) + (LANES - AUG)
    )
    select = jnp.where(jnp.logical_and(pick, jnp.logical_not(head_rows)), 1.0, 0.0).astype(BF16)
    top_rows = lax.broadcasted_iota(jnp.int32, (AUG, CHUNK), 0) < AUG - HEAD
    keep = lax.broadcasted_iota(jnp.int32, (CHUNK, LANES), 1) < HEAD

    def chunk(side, o):
        return chunks[side, o].reshape(CHUNK, LANES)

    def prepare(side, o):
        t = lax.dot_general(select, chunk(side, o), NT, preferred_element_type=F32)
        uts[side, o] = jnp.where(top_rows, 1.0, t).astype(BF16)
        queries[side, o] = jnp.where(keep, chunk(side, o), jnp.zeros((), BF16))

    def scores(side, mine, half, others, buf):
        query = queries[side, mine, half * BLK:(half + 1) * BLK]
        top = None
        for k, other in enumerate(others):
            s = lax.dot_general(chunk(1 - side, other), query, NT, preferred_element_type=F32)
            buf[k] = s
            t = jnp.max(s, axis=0, keepdims=True)
            top = t if top is None else jnp.maximum(top, t)
        return top

    def weigh(side, mine, half, others, buf, top, fresh):
        cols = slice(half * BLK, (half + 1) * BLK)
        acc = None
        if not fresh:
            old = tops[side, mine, 0:1, cols]
            top = jnp.maximum(top, old)
            acc = accs[side, mine, :, cols] * jnp.exp2((old - top) * C2)
        for k, other in enumerate(others):
            w = jnp.exp2((buf[k] - top) * C2).astype(BF16)
            term = jnp.dot(uts[1 - side, other], w, preferred_element_type=F32)
            acc = term if acc is None else acc + term
        return acc, top

    def publish(side, o):
        there = MIRROR[o]
        pltpu.make_async_remote_copy(
            src_ref=num_out.at[side, o], dst_ref=num_in.at[side, there],
            send_sem=n_send.at[side, o], recv_sem=n_recv.at[side, there],
            device_id=peers[side](shift_xy(o)), device_id_type=MESH,
        ).start()
        pltpu.make_async_remote_copy(
            src_ref=st_out.at[side, o], dst_ref=st_in.at[side, there],
            send_sem=t_send.at[side, o], recv_sem=t_recv.at[side, there],
            device_id=peers[side](shift_xy(o)), device_id_type=MESH,
        ).start()

    def store(side, mine, half, acc, top, last):
        cols = slice(half * BLK, (half + 1) * BLK)
        if last:
            num_out[side, mine, :, cols] = acc[AUG - HEAD:].astype(BF16)
            st_out[side, mine, 0:8, cols] = acc[0:8]
            st_out[side, mine, 8:16, cols] = jnp.broadcast_to(top, (8, BLK))
            if mine and half:
                publish(side, mine)
        else:
            accs[side, mine, :, cols] = acc
            tops[side, mine, :, cols] = jnp.broadcast_to(top, (8, BLK))

    bufs = (sbuf_a, sbuf_b)
    for wave in range(NX):
        if wave:
            for group in range(2):
                for side in range(2):
                    gathered(side, group, wave).wait()
        prepare(0, wave)
        prepare(1, wave)
        last = wave == NX - 1
        units = []
        for side in range(2):
            for mine in range(1, wave):
                units += [(side, mine, half, (wave,)) for half in range(2)]
            units += [(side, wave, half, tuple(range(wave + 1))) for half in range(2)]
        if wave:
            units += [(side, 0, half, (wave,)) for side in range(2) for half in range(2)]
        top = scores(*units[0], bufs[0])
        for n, unit in enumerate(units):
            following = None
            if n + 1 < len(units):
                following = scores(*units[n + 1], bufs[(n + 1) % 2])
            acc, top = weigh(*unit, bufs[n % 2], top, unit[1] == wave)
            store(*unit[:3], acc, top, last)
            top = following

    def combine(side):
        for o in (1, 2, 3):
            pltpu.make_async_remote_copy(
                src_ref=num_out.at[side, o], dst_ref=num_in.at[side, o],
                send_sem=n_send.at[side, o], recv_sem=n_recv.at[side, o],
                device_id=peers[side](shift_xy(o)), device_id_type=MESH,
            ).wait()
            pltpu.make_async_remote_copy(
                src_ref=st_out.at[side, o], dst_ref=st_in.at[side, o],
                send_sem=t_send.at[side, o], recv_sem=t_recv.at[side, o],
                device_id=peers[side](shift_xy(o)), device_id_type=MESH,
            ).wait()
        nums = [num_out[side, 0]] + [num_in[side, o] for o in (1, 2, 3)]
        stats = [st_out[side, 0]] + [st_in[side, o] for o in (1, 2, 3)]
        highs = [s[8:9] for s in stats]
        top = jnp.maximum(jnp.maximum(highs[0], highs[1]), jnp.maximum(highs[2], highs[3]))
        total = jnp.zeros((1, CHUNK), F32)
        mixed = jnp.zeros((HEAD, CHUNK), F32)
        for o in range(NX):
            fade = jnp.exp2((highs[o] - top) * C2)
            total = total + stats[o][0:1] * fade
            mixed = mixed + nums[o].astype(F32) * fade
        attn = mixed / total
        pair = jnp.concatenate([attn, pltpu.roll(attn, CHUNK - ROWS // 2, 1)], axis=0)
        a_out[side] = pair.T.astype(BF16).reshape(NP, ROWS, LANES)[:, :ROWS // 2]

        def send_back(d, _):
            s = (core + d) % NP
            q = (z + shift_z(s // 2) + HALF) % HALF * 2 + s % 2
            pltpu.make_async_remote_copy(
                src_ref=a_out.at[side, s], dst_ref=a_in.at[side, p],
                send_sem=r_send.at[side, q], recv_sem=r_recv.at[side, p],
                device_id=zc_peer(q), device_id_type=MESH,
            ).start()
            return 0

        lax.fori_loop(1, NP, send_back, 0)
        a_in[side, p] = a_out[side, core]

    def wait_back(side):
        def wait(d, _):
            q = (p + d) % NP
            pltpu.make_async_remote_copy(
                src_ref=a_out.at[side, 0], dst_ref=a_in.at[side, q],
                send_sem=r_send.at[side, q], recv_sem=r_recv.at[side, q],
                device_id=zc_peer(q), device_id_type=MESH,
            ).wait()
            return 0

        lax.fori_loop(1, NP, wait, 0)

    half_low = low[:ROWS // 2]

    def finish(side, gain):
        wait_back(side)
        parts = []
        for k in range(H // 2):
            a = a_in[side, 2 * k].astype(F32)
            b = a_in[side, 2 * k + 1].astype(F32)
            upper = jnp.where(half_low, a, pltpu.roll(b, HEAD, 1))
            lower = jnp.where(half_low, pltpu.roll(a, HEAD, 1), b)
            parts.append(jnp.concatenate([upper, lower], axis=0))
        mixed = jnp.concatenate(parts, axis=1)
        power = jnp.mean(mixed * mixed, axis=-1, keepdims=True)
        normed = (mixed * lax.rsqrt(power + 1e-6) * gain[...]).astype(BF16)
        update = jnp.dot(normed, wbuf[4 + side], preferred_element_type=F32)
        update_out[side * ROWS:(side + 1) * ROWS] = update

    combine(0)
    loads[4].wait()
    loads[5].wait()
    combine(1)
    finish(0, s_gain)
    finish(1, v_gain)


def local(sensor, video, w_sr, w_vr, w_su, w_vu, w_so, w_vo, s_gain, v_gain):
    vmem = pl.BlockSpec(memory_space=pltpu.VMEM)
    hbm = pl.BlockSpec(memory_space=pl.ANY)
    dma = pltpu.SemaphoreType.DMA
    update = pl.pallas_call(
        kernel,
        out_shape=jax.ShapeDtypeStruct((2 * ROWS, D), F32),
        in_specs=[vmem, vmem] + [hbm] * 6 + [vmem, vmem],
        out_specs=vmem,
        scratch_shapes=[
            pltpu.VMEM((6, D, D), BF16),
            pltpu.VMEM((2, NP, ROWS, LANES), BF16),
            pltpu.VMEM((2, NX, NP, ROWS, LANES), BF16),
            pltpu.VMEM((2, NX, AUG, CHUNK), BF16),
            pltpu.VMEM((2, NX, HEAD, CHUNK), BF16),
            pltpu.VMEM((2, NX, 16, CHUNK), F32),
            pltpu.VMEM((2, NX, HEAD, CHUNK), BF16),
            pltpu.VMEM((2, NX, 16, CHUNK), F32),
            pltpu.VMEM((2, NP, ROWS // 2, LANES), BF16),
            pltpu.VMEM((2, NP, ROWS // 2, LANES), BF16),
            pltpu.VMEM((2, NX, CHUNK, LANES), BF16),
            pltpu.VMEM((2, NX, AUG, CHUNK), F32),
            pltpu.VMEM((2, NX, 8, CHUNK), F32),
            pltpu.VMEM((NX, CHUNK, BLK), F32),
            pltpu.VMEM((NX, CHUNK, BLK), F32),
            dma((6,)),
            dma((2, NP)), dma((2, NP)),
            dma((2, 2, NX)), dma((2, 2, NX)),
            dma((2, NX)), dma((2, NX)),
            dma((2, NX)), dma((2, NX)),
            dma((2, NP)), dma((2, NP)),
        ],
        compiler_params=pltpu.CompilerParams(
            collective_id=0, has_side_effects=True, vmem_limit_bytes=60 * 1024 * 1024
        ),
    )(
        sensor, video, w_sr, w_vr, w_su, w_vu, w_so, w_vo,
        s_gain.reshape(1, D), v_gain.reshape(1, D),
    )
    return (
        (sensor.astype(F32) + update[:ROWS]).astype(BF16),
        (video.astype(F32) + update[ROWS:]).astype(BF16),
    )


def solution(mesh):
    rows = P(("blk", "quarter"), None)
    return jax.shard_map(
        local,
        mesh=mesh,
        in_specs=(rows, rows) + (P(),) * 8,
        out_specs=(rows, rows),
        check_vma=False,
    )
```

```python
import functools
import math

import jax
import jax.numpy as jnp
from jax import lax
from jax.experimental import pallas as pl
from jax.experimental.pallas import tpu as pltpu
from jax.sharding import PartitionSpec as P

H = 16
MESH = pl.DeviceIdType.MESH
F32 = jnp.float32
BF16 = jnp.bfloat16
NX = 4
NY = 4
NP = 16
ROWS = 32
D = 1024
LANES = 128
HEAD = 64
CHUNK = NP * ROWS
TOK = NX * CHUNK
NT = (((1,), (1,)), ((), ()))
C2 = math.log2(math.e) * HEAD ** -0.5
AUG = 80
BLK = 256
HALF = NP // 2
GROUPS = ((0, 8), (8, 4), (12, 4))


def shift_z(t):
    return (t % 2) * ((t + 1) // 2) - (1 - t % 2) * (t // 2)


def shift_xy(o):
    return o + o // 2 - 2 * (o // 3)


MIRROR = (0, 2, 1, 3)


def kernel(
    sensor, video, w_sr, w_vr, w_su, w_vu, w_so, w_vo, s_gain, v_gain,
    update_out,
    wbuf, stage, chunks, s_ut, num_out, st_out, num_in, st_in, a_out, a_in, v_ref, v_val, v_acc, v_top, s_acc, s_top, sbuf_a, sbuf_b, k0, k1, k2, k3, k4, k5,
    w_sem, z_send, z_recv, g_send, g_recv, n_send, n_recv, t_send, t_recv, r_send, r_recv,
):
    blk = lax.axis_index("blk")
    quarter = lax.axis_index("quarter")
    core = blk % 2
    x_lo = (blk // 2) % 2
    z = blk // 4
    x_hi = quarter % 2
    y = quarter // 2
    x = x_hi * 2 + x_lo
    p = z * 2 + core

    def zc_peer(q):
        return (((q // 2) * 2 + x_lo) * 2 + q % 2, quarter)

    def x_peer(d):
        k = (x + d) % NX
        return ((z * 2 + k % 2) * 2 + core, y * 2 + k // 2)

    def y_peer(d):
        return (blk, (y + d) % NY * 2 + x_hi)

    peers = (x_peer, y_peer)
    weights = (w_sr, w_su, w_vr, w_vu, w_so, w_vo)
    loads = [pltpu.make_async_copy(w, wbuf.at[k], w_sem.at[k]) for k, w in enumerate(weights)]
    for load in loads:
        load.start()

    barrier = pltpu.get_barrier_semaphore()

    def greet_zc(d, _):
        pl.semaphore_signal(barrier, inc=1, device_id=zc_peer((p + d) % NP), device_id_type=MESH)
        return 0

    def greet_xy(d, _):
        pl.semaphore_signal(barrier, inc=1, device_id=x_peer(d), device_id_type=MESH)
        pl.semaphore_signal(barrier, inc=1, device_id=y_peer(d), device_id_type=MESH)
        return 0

    lax.fori_loop(1, NP, greet_zc, 0)
    lax.fori_loop(1, NX, greet_xy, 0)

    low = lax.broadcasted_iota(jnp.int32, (ROWS, LANES), 1) < HEAD

    def project(rows, first, side):
        loads[first].wait()
        ref = jnp.dot(rows[...], wbuf[first], preferred_element_type=F32)
        loads[first + 1].wait()
        val = jnp.dot(rows[...], wbuf[first + 1], preferred_element_type=F32)
        for k in range(H // 2):
            a = ref[:, k * LANES:(k + 1) * LANES]
            b = val[:, k * LANES:(k + 1) * LANES]
            stage[side, 2 * k] = jnp.where(low, a, pltpu.roll(b, HEAD, 1)).astype(BF16)
            stage[side, 2 * k + 1] = jnp.where(low, pltpu.roll(a, HEAD, 1), b).astype(BF16)

    def head_copy(side, s, sender):
        t = s // 2
        sign = -1 if sender else 1
        q = (z + sign * shift_z(t) + HALF) % HALF * 2 + s % 2
        return pltpu.make_async_remote_copy(
            src_ref=stage.at[side, q],
            dst_ref=chunks.at[side, 0, t * 2 + core if sender else s],
            send_sem=z_send.at[side, s],
            recv_sem=z_recv.at[side, t * 2 + core if sender else s],
            device_id=zc_peer(q), device_id_type=MESH,
        )

    def send_heads(side, group):
        def send(d, _):
            first, size = GROUPS[group]
            s = (core + d) % size if group == 0 else first + d
            head_copy(side, s, True).start()
            return 0

        lax.fori_loop(1 if group == 0 else 0, GROUPS[group][1], send, 0)
        if group == 0:
            chunks[side, 0, core] = stage[side, p]

    def await_heads(side, group):
        def wait(d, _):
            first, size = GROUPS[group]
            s = (core + d) % size if group == 0 else first + d
            head_copy(side, s, False).wait()
            return 0

        lax.fori_loop(1 if group == 0 else 0, GROUPS[group][1], wait, 0)

    def gather_copy(side, group, o):
        part = pl.ds(*GROUPS[group])
        return pltpu.make_async_remote_copy(
            src_ref=chunks.at[side, 0, part], dst_ref=chunks.at[side, MIRROR[o], part],
            send_sem=g_send.at[side, group, o], recv_sem=g_recv.at[side, group, MIRROR[o]],
            device_id=peers[side](shift_xy(o)), device_id_type=MESH,
        )

    def gathered(side, group, o):
        part = pl.ds(*GROUPS[group])
        return pltpu.make_async_remote_copy(
            src_ref=chunks.at[side, 0, part], dst_ref=chunks.at[side, o, part],
            send_sem=g_send.at[side, group, o], recv_sem=g_recv.at[side, group, o],
            device_id=peers[side](shift_xy(o)), device_id_type=MESH,
        )

    project(sensor, 0, 0)
    project(video, 2, 1)
    pl.semaphore_wait(barrier, (NP - 1) + (NX - 1) + (NY - 1))
    for group in range(len(GROUPS)):
        for side in range(2):
            send_heads(side, group)
    for group in range(len(GROUPS)):
        for side in range(2):
            await_heads(side, group)
            for o in (1, 2):
                gather_copy(side, group, o).start()
    for group in range(len(GROUPS)):
        for side in range(2):
            gather_copy(side, group, 3).start()

    head_rows = lax.broadcasted_iota(jnp.int32, (AUG, LANES), 0) < AUG - HEAD
    pick = (
        lax.broadcasted_iota(jnp.int32, (AUG, LANES), 1)
        == lax.broadcasted_iota(jnp.int32, (AUG, LANES), 0) + (LANES - AUG)
    )
    select = jnp.where(jnp.logical_and(pick, jnp.logical_not(head_rows)), 1.0, 0.0).astype(BF16)
    top_rows = lax.broadcasted_iota(jnp.int32, (AUG, CHUNK), 0) < AUG - HEAD
    keep = lax.broadcasted_iota(jnp.int32, (CHUNK, LANES), 1) < HEAD

    def chunk(side, o):
        return chunks[side, o].reshape(CHUNK, LANES)

    def prepare(o):
        t = lax.dot_general(select, chunk(0, o), NT, preferred_element_type=F32)
        s_ut[o] = jnp.where(top_rows, 1.0, t).astype(BF16)
        v_ref[o] = jnp.where(keep, chunk(1, o), jnp.zeros((), BF16))
        v_val[o] = jnp.where(keep, jnp.ones((), BF16), chunk(1, o))

    halves = [slice(half * BLK, (half + 1) * BLK) for half in range(CHUNK // BLK)]

    def scores(a, b, buf):
        cols, rows = [], None
        for n, part in enumerate(halves):
            s = lax.dot_general(chunk(0, a), v_ref[b, part], NT, preferred_element_type=F32)
            buf[n] = s
            cols.append(jnp.max(s, axis=0, keepdims=True))
            r = jnp.maximum(s[:, :LANES], s[:, LANES:])
            rows = r if rows is None else jnp.maximum(rows, r)
        rows = jnp.broadcast_to(jnp.max(rows, axis=1, keepdims=True), (CHUNK, LANES))
        return cols, rows

    def publish(side, o):
        there = MIRROR[o]
        pltpu.make_async_remote_copy(
            src_ref=num_out.at[side, o], dst_ref=num_in.at[side, there],
            send_sem=n_send.at[side, o], recv_sem=n_recv.at[side, there],
            device_id=peers[side](shift_xy(o)), device_id_type=MESH,
        ).start()
        pltpu.make_async_remote_copy(
            src_ref=st_out.at[side, o], dst_ref=st_in.at[side, there],
            send_sem=t_send.at[side, o], recv_sem=t_recv.at[side, there],
            device_id=peers[side](shift_xy(o)), device_id_type=MESH,
        ).start()

    first_row = lax.broadcasted_iota(jnp.int32, (8, BLK), 0) == 0
    top_lane = lax.broadcasted_iota(jnp.int32, (CHUNK, LANES), 1) == 1

    def weigh_video(a, b, buf, cols, fresh, last):
        for n, part in enumerate(halves):
            top = cols[n]
            if not fresh:
                old = v_top[b, 0:1, part]
                top = jnp.maximum(top, old)
            w = jnp.exp2((buf[n] - top) * C2).astype(BF16)
            acc = jnp.dot(s_ut[a], w, preferred_element_type=F32)
            if not fresh:
                acc = acc + v_acc[b, :, part] * jnp.exp2((old - top) * C2)
            if last:
                num_out[1, b, :, part] = acc[AUG - HEAD:].astype(BF16)
                st_out[1, b, :, part] = jnp.where(first_row, acc[0:8], top)
            else:
                v_acc[b, :, part] = acc
                v_top[b, :, part] = jnp.broadcast_to(top, (8, BLK))
        if last and b:
            publish(1, b)

    def weigh_sensor(a, b, buf, top, fresh, last):
        if not fresh:
            old = s_top[a]
            top = jnp.maximum(top, old)
        wide = jnp.concatenate([top] * (BLK // LANES), axis=1)
        acc = None
        for n, part in enumerate(halves):
            w = jnp.exp2((buf[n] - wide) * C2).astype(BF16)
            term = jnp.dot(w, v_val[b, part], preferred_element_type=F32)
            acc = term if acc is None else acc + term
        if not fresh:
            acc = acc + s_acc[a] * jnp.exp2((old - top) * C2)
        if last:
            t = jnp.where(top_lane, top, acc).T
            num_out[0, a] = t[HEAD:].astype(BF16)
            st_out[0, a] = t[:8]
            if a:
                publish(0, a)
        else:
            s_acc[a] = acc
            s_top[a] = top

    bufs = (sbuf_a, sbuf_b)
    kept = (k0, k1, k2, k3, k4, k5)
    later = []
    s_count, v_count = [0] * NX, [0] * NX
    for wave in range(NX):
        if wave:
            for group in range(len(GROUPS)):
                for side in range(2):
                    gathered(side, group, wave).wait()
        prepare(wave)
        tiles = []
        for o in list(range(1, wave)) + ([0] if wave else []):
            tiles += [(wave, o), (o, wave)]
        tiles.append((wave, wave))
        places = []
        for n, (a, b) in enumerate(tiles):
            own = (a == 0) != (b == 0)
            places.append(kept[2 * (a + b - 1) + (a == 0)] if own else bufs[n % 2])
        tops = scores(*tiles[0], places[0])
        for n, (a, b) in enumerate(tiles):
            following = None
            if n + 1 < len(tiles):
                following = scores(*tiles[n + 1], places[n + 1])
            if b or not a:
                weigh_video(a, b, places[n], tops[0], v_count[b] == 0, v_count[b] == NX - 1)
                v_count[b] += 1
            else:
                later.append((weigh_video, a, b, places[n], tops[0]))
            if a or not b:
                weigh_sensor(a, b, places[n], tops[1], s_count[a] == 0, s_count[a] == NX - 1)
                s_count[a] += 1
            else:
                later.append((weigh_sensor, a, b, places[n], tops[1]))
            tops = following
    for part, a, b, place, top in later:
        part(a, b, place, top, False, a + b == NX - 1)

    def combine(side):
        for o in (1, 2, 3):
            pltpu.make_async_remote_copy(
                src_ref=num_out.at[side, o], dst_ref=num_in.at[side, o],
                send_sem=n_send.at[side, o], recv_sem=n_recv.at[side, o],
                device_id=peers[side](shift_xy(o)), device_id_type=MESH,
            ).wait()
            pltpu.make_async_remote_copy(
                src_ref=st_out.at[side, o], dst_ref=st_in.at[side, o],
                send_sem=t_send.at[side, o], recv_sem=t_recv.at[side, o],
                device_id=peers[side](shift_xy(o)), device_id_type=MESH,
            ).wait()
        nums = [num_out[side, 0]] + [num_in[side, o] for o in (1, 2, 3)]
        stats = [st_out[side, 0]] + [st_in[side, o] for o in (1, 2, 3)]
        highs = [s[1:2] for s in stats]
        top = jnp.maximum(jnp.maximum(highs[0], highs[1]), jnp.maximum(highs[2], highs[3]))
        total = jnp.zeros((1, CHUNK), F32)
        mixed = jnp.zeros((HEAD, CHUNK), F32)
        for o in range(NX):
            fade = jnp.exp2((highs[o] - top) * C2)
            total = total + stats[o][0:1] * fade
            mixed = mixed + nums[o].astype(F32) * fade
        attn = mixed / total
        pair = jnp.concatenate([attn, pltpu.roll(attn, CHUNK - ROWS // 2, 1)], axis=0)
        a_out[side] = pair.T.astype(BF16).reshape(NP, ROWS, LANES)[:, :ROWS // 2]

        def send_back(d, _):
            s = (core + NP - d) % NP
            q = (z + shift_z(s // 2) + HALF) % HALF * 2 + s % 2
            pltpu.make_async_remote_copy(
                src_ref=a_out.at[side, s], dst_ref=a_in.at[side, p],
                send_sem=r_send.at[side, q], recv_sem=r_recv.at[side, p],
                device_id=zc_peer(q), device_id_type=MESH,
            ).start()
            return 0

        lax.fori_loop(1, NP, send_back, 0)
        a_in[side, p] = a_out[side, core]

    def wait_back(side):
        def wait(d, _):
            q = (p + d) % NP
            pltpu.make_async_remote_copy(
                src_ref=a_out.at[side, 0], dst_ref=a_in.at[side, q],
                send_sem=r_send.at[side, q], recv_sem=r_recv.at[side, q],
                device_id=zc_peer(q), device_id_type=MESH,
            ).wait()
            return 0

        lax.fori_loop(1, NP, wait, 0)

    half_low = low[:ROWS // 2]

    def finish(side, gain):
        wait_back(side)
        parts = []
        for k in range(H // 2):
            a = a_in[side, 2 * k].astype(F32)
            b = a_in[side, 2 * k + 1].astype(F32)
            upper = jnp.where(half_low, a, pltpu.roll(b, HEAD, 1))
            lower = jnp.where(half_low, pltpu.roll(a, HEAD, 1), b)
            parts.append(jnp.concatenate([upper, lower], axis=0))
        mixed = jnp.concatenate(parts, axis=1)
        power = jnp.mean(mixed * mixed, axis=-1, keepdims=True)
        normed = (mixed * lax.rsqrt(power + 1e-6) * gain[...]).astype(BF16)
        update = jnp.dot(normed, wbuf[4 + side], preferred_element_type=F32)
        update_out[side * ROWS:(side + 1) * ROWS] = update

    combine(0)
    loads[4].wait()
    loads[5].wait()
    combine(1)
    finish(0, s_gain)
    finish(1, v_gain)


def local(sensor, video, w_sr, w_vr, w_su, w_vu, w_so, w_vo, s_gain, v_gain):
    vmem = pl.BlockSpec(memory_space=pltpu.VMEM)
    hbm = pl.BlockSpec(memory_space=pl.ANY)
    dma = pltpu.SemaphoreType.DMA
    update = pl.pallas_call(
        kernel,
        out_shape=jax.ShapeDtypeStruct((2 * ROWS, D), F32),
        in_specs=[vmem, vmem] + [hbm] * 6 + [vmem, vmem],
        out_specs=vmem,
        scratch_shapes=[
            pltpu.VMEM((6, D, D), BF16),
            pltpu.VMEM((2, NP, ROWS, LANES), BF16),
            pltpu.VMEM((2, NX, NP, ROWS, LANES), BF16),
            pltpu.VMEM((NX, AUG, CHUNK), BF16),
            pltpu.VMEM((2, NX, HEAD, CHUNK), BF16),
            pltpu.VMEM((2, NX, 8, CHUNK), F32),
            pltpu.VMEM((2, NX, HEAD, CHUNK), BF16),
            pltpu.VMEM((2, NX, 8, CHUNK), F32),
            pltpu.VMEM((2, NP, ROWS // 2, LANES), BF16),
            pltpu.VMEM((2, NP, ROWS // 2, LANES), BF16),
            pltpu.VMEM((NX, CHUNK, LANES), BF16),
            pltpu.VMEM((NX, CHUNK, LANES), BF16),
            pltpu.VMEM((NX, AUG, CHUNK), F32),
            pltpu.VMEM((NX, 8, CHUNK), F32),
            pltpu.VMEM((NX, CHUNK, LANES), F32),
            pltpu.VMEM((NX, CHUNK, LANES), F32),
            pltpu.VMEM((2, CHUNK, BLK), F32),
            pltpu.VMEM((2, CHUNK, BLK), F32),
            pltpu.VMEM((2, CHUNK, BLK), F32),
            pltpu.VMEM((2, CHUNK, BLK), F32),
            pltpu.VMEM((2, CHUNK, BLK), F32),
            pltpu.VMEM((2, CHUNK, BLK), F32),
            pltpu.VMEM((2, CHUNK, BLK), F32),
            pltpu.VMEM((2, CHUNK, BLK), F32),
            dma((6,)),
            dma((2, NP)), dma((2, NP)),
            dma((2, len(GROUPS), NX)), dma((2, len(GROUPS), NX)),
            dma((2, NX)), dma((2, NX)),
            dma((2, NX)), dma((2, NX)),
            dma((2, NP)), dma((2, NP)),
        ],
        compiler_params=pltpu.CompilerParams(
            collective_id=0, has_side_effects=True, vmem_limit_bytes=60 * 1024 * 1024
        ),
    )(
        sensor, video, w_sr, w_vr, w_su, w_vu, w_so, w_vo,
        s_gain.reshape(1, D), v_gain.reshape(1, D),
    )
    return (
        (sensor.astype(F32) + update[:ROWS]).astype(BF16),
        (video.astype(F32) + update[ROWS:]).astype(BF16),
    )


def solution(mesh):
    rows = P(("blk", "quarter"), None)
    return jax.shard_map(
        local,
        mesh=mesh,
        in_specs=(rows, rows) + (P(),) * 8,
        out_specs=(rows, rows),
        check_vma=False,
    )
```

```python
import functools
import math

import jax
import jax.numpy as jnp
from jax import lax
from jax.experimental import pallas as pl
from jax.experimental.pallas import tpu as pltpu
from jax.sharding import PartitionSpec as P

H = 16
MESH = pl.DeviceIdType.MESH
F32 = jnp.float32
BF16 = jnp.bfloat16
NX = 4
NY = 4
NP = 16
ROWS = 32
D = 1024
LANES = 128
HEAD = 64
CHUNK = NP * ROWS
TOK = NX * CHUNK
NT = (((1,), (1,)), ((), ()))
C2 = math.log2(math.e) * HEAD ** -0.5
AUG = 80
BLK = 256
HALF = NP // 2
GROUPS = ((0, 8), (8, 4), (12, 4))


def shift_z(t):
    return (t % 2) * ((t + 1) // 2) - (1 - t % 2) * (t // 2)


def shift_xy(o):
    return o + o // 2 - 2 * (o // 3)


MIRROR = (0, 2, 1, 3)


def kernel(
    sensor, video, w_sr, w_vr, w_su, w_vu, w_so, w_vo, s_gain, v_gain,
    update_out,
    wbuf, stage, chunks, s_ut, num_out, st_out, num_in, st_in, a_out, a_in, v_ref, v_val, v_acc, v_top, s_acc, s_top, sbuf_a, sbuf_b, k0, k1, k2, k3, k4, k5,
    w_sem, z_send, z_recv, g_send, g_recv, n_send, n_recv, t_send, t_recv, r_send, r_recv,
):
    blk = lax.axis_index("blk")
    quarter = lax.axis_index("quarter")
    core = blk % 2
    x_lo = (blk // 2) % 2
    z = blk // 4
    x_hi = quarter % 2
    y = quarter // 2
    x = x_hi * 2 + x_lo
    p = z * 2 + core

    def zc_peer(q):
        return (((q // 2) * 2 + x_lo) * 2 + q % 2, quarter)

    def x_peer(d):
        k = (x + d) % NX
        return ((z * 2 + k % 2) * 2 + core, y * 2 + k // 2)

    def y_peer(d):
        return (blk, (y + d) % NY * 2 + x_hi)

    peers = (x_peer, y_peer)
    weights = (w_sr, w_su, w_vr, w_vu, w_so, w_vo)
    loads = [pltpu.make_async_copy(w, wbuf.at[k], w_sem.at[k]) for k, w in enumerate(weights)]
    for load in loads:
        load.start()

    barrier = pltpu.get_barrier_semaphore()

    def greet_zc(d, _):
        pl.semaphore_signal(barrier, inc=1, device_id=zc_peer((p + d) % NP), device_id_type=MESH)
        return 0

    def greet_xy(d, _):
        pl.semaphore_signal(barrier, inc=1, device_id=x_peer(d), device_id_type=MESH)
        pl.semaphore_signal(barrier, inc=1, device_id=y_peer(d), device_id_type=MESH)
        return 0

    lax.fori_loop(1, NP, greet_zc, 0)
    lax.fori_loop(1, NX, greet_xy, 0)

    low = lax.broadcasted_iota(jnp.int32, (ROWS, LANES), 1) < HEAD

    def project(rows, first, side):
        loads[first].wait()
        ref = jnp.dot(rows[...], wbuf[first], preferred_element_type=F32)
        loads[first + 1].wait()
        val = jnp.dot(rows[...], wbuf[first + 1], preferred_element_type=F32)
        for k in range(H // 2):
            a = ref[:, k * LANES:(k + 1) * LANES]
            b = val[:, k * LANES:(k + 1) * LANES]
            stage[side, 2 * k] = jnp.where(low, a, pltpu.roll(b, HEAD, 1)).astype(BF16)
            stage[side, 2 * k + 1] = jnp.where(low, pltpu.roll(a, HEAD, 1), b).astype(BF16)

    def head_copy(side, s, sender):
        t = s // 2
        sign = -1 if sender else 1
        there = (z + sign * shift_z(t) + HALF) % HALF
        q = there * 2 + s % 2
        return pltpu.make_async_remote_copy(
            src_ref=stage.at[side, q],
            dst_ref=chunks.at[side, 0, t * 2 + core if sender else s],
            send_sem=z_send.at[side, s],
            recv_sem=z_recv.at[side, t * 2 + core if sender else s],
            device_id=(there * 4 + x_lo * 2 + s % 2, quarter), device_id_type=MESH,
        )

    def send_heads(side, group):
        first, size = GROUPS[group]
        if group == 0:
            head_copy(side, 1 - core, True).start()
        for s in range(2 if group == 0 else first, first + size):
            head_copy(side, s, True).start()
        if group == 0:
            chunks[side, 0, core] = stage[side, p]

    def await_heads(side, group):
        def wait(d, _):
            first, size = GROUPS[group]
            s = (core + d) % size if group == 0 else first + d
            head_copy(side, s, False).wait()
            return 0

        lax.fori_loop(1 if group == 0 else 0, GROUPS[group][1], wait, 0)

    def gather_copy(side, group, o):
        part = pl.ds(*GROUPS[group])
        return pltpu.make_async_remote_copy(
            src_ref=chunks.at[side, 0, part], dst_ref=chunks.at[side, MIRROR[o], part],
            send_sem=g_send.at[side, group, o], recv_sem=g_recv.at[side, group, MIRROR[o]],
            device_id=peers[side](shift_xy(o)), device_id_type=MESH,
        )

    def gathered(side, group, o):
        part = pl.ds(*GROUPS[group])
        return pltpu.make_async_remote_copy(
            src_ref=chunks.at[side, 0, part], dst_ref=chunks.at[side, o, part],
            send_sem=g_send.at[side, group, o], recv_sem=g_recv.at[side, group, o],
            device_id=peers[side](shift_xy(o)), device_id_type=MESH,
        )

    project(sensor, 0, 0)
    project(video, 2, 1)
    pl.semaphore_wait(barrier, (NP - 1) + (NX - 1) + (NY - 1))
    for group in range(len(GROUPS)):
        for side in range(2):
            send_heads(side, group)
    for group in range(len(GROUPS)):
        for side in range(2):
            await_heads(side, group)
            for o in (1, 2):
                gather_copy(side, group, o).start()
    for group in range(len(GROUPS)):
        for side in range(2):
            gather_copy(side, group, 3).start()

    head_rows = lax.broadcasted_iota(jnp.int32, (AUG, LANES), 0) < AUG - HEAD
    pick = (
        lax.broadcasted_iota(jnp.int32, (AUG, LANES), 1)
        == lax.broadcasted_iota(jnp.int32, (AUG, LANES), 0) + (LANES - AUG)
    )
    select = jnp.where(jnp.logical_and(pick, jnp.logical_not(head_rows)), 1.0, 0.0).astype(BF16)
    top_rows = lax.broadcasted_iota(jnp.int32, (AUG, CHUNK), 0) < AUG - HEAD
    keep = lax.broadcasted_iota(jnp.int32, (CHUNK, LANES), 1) < HEAD

    def chunk(side, o):
        return chunks[side, o].reshape(CHUNK, LANES)

    def prepare(o):
        t = lax.dot_general(select, chunk(0, o), NT, preferred_element_type=F32)
        s_ut[o] = jnp.where(top_rows, 1.0, t).astype(BF16)
        v_ref[o] = jnp.where(keep, chunk(1, o), jnp.zeros((), BF16))
        v_val[o] = jnp.where(keep, jnp.ones((), BF16), chunk(1, o))

    halves = [slice(half * BLK, (half + 1) * BLK) for half in range(CHUNK // BLK)]

    def scores(a, b, buf):
        cols, rows = [], None
        for n, part in enumerate(halves):
            s = lax.dot_general(chunk(0, a), v_ref[b, part], NT, preferred_element_type=F32)
            buf[n] = s
            cols.append(jnp.max(s, axis=0, keepdims=True))
            r = jnp.maximum(s[:, :LANES], s[:, LANES:])
            rows = r if rows is None else jnp.maximum(rows, r)
        rows = jnp.broadcast_to(jnp.max(rows, axis=1, keepdims=True), (CHUNK, LANES))
        return cols, rows

    def publish(side, o):
        there = MIRROR[o]
        pltpu.make_async_remote_copy(
            src_ref=num_out.at[side, o], dst_ref=num_in.at[side, there],
            send_sem=n_send.at[side, o], recv_sem=n_recv.at[side, there],
            device_id=peers[side](shift_xy(o)), device_id_type=MESH,
        ).start()
        pltpu.make_async_remote_copy(
            src_ref=st_out.at[side, o], dst_ref=st_in.at[side, there],
            send_sem=t_send.at[side, o], recv_sem=t_recv.at[side, there],
            device_id=peers[side](shift_xy(o)), device_id_type=MESH,
        ).start()

    top_lane = lax.broadcasted_iota(jnp.int32, (CHUNK, LANES), 1) == 1

    def weigh_video(a, b, buf, cols, fresh, last):
        for n, part in enumerate(halves):
            top = cols[n]
            if not fresh:
                old = v_top[b, 0:1, part]
                top = jnp.maximum(top, old)
            w = jnp.exp2((buf[n] - top) * C2).astype(BF16)
            acc = jnp.dot(s_ut[a], w, preferred_element_type=F32)
            if not fresh:
                acc = acc + v_acc[b, :, part] * jnp.exp2((old - top) * C2)
            if last:
                num_out[1, b, :, part] = acc[AUG - HEAD:].astype(BF16)
                for k in range(BLK // LANES):
                    row = n * (BLK // LANES) + k
                    st_out[1, b, row:row + 1] = acc[0:1, k * LANES:(k + 1) * LANES]
                    st_out[1, b, row + 4:row + 5] = top[:, k * LANES:(k + 1) * LANES]
            else:
                v_acc[b, :, part] = acc
                v_top[b, :, part] = jnp.broadcast_to(top, (8, BLK))
        if last and b:
            publish(1, b)

    def weigh_sensor(a, b, buf, top, fresh, last):
        if not fresh:
            old = s_top[a]
            top = jnp.maximum(top, old)
        wide = jnp.concatenate([top] * (BLK // LANES), axis=1)
        acc = None
        for n, part in enumerate(halves):
            w = jnp.exp2((buf[n] - wide) * C2).astype(BF16)
            term = jnp.dot(w, v_val[b, part], preferred_element_type=F32)
            acc = term if acc is None else acc + term
        if not fresh:
            acc = acc + s_acc[a] * jnp.exp2((old - top) * C2)
        if last:
            t = jnp.where(top_lane, top, acc).T
            num_out[0, a] = t[HEAD:].astype(BF16)
            for k in range(CHUNK // LANES):
                st_out[0, a, k:k + 1] = t[0:1, k * LANES:(k + 1) * LANES]
                st_out[0, a, k + 4:k + 5] = t[1:2, k * LANES:(k + 1) * LANES]
            if a:
                publish(0, a)
        else:
            s_acc[a] = acc
            s_top[a] = top

    bufs = (sbuf_a, sbuf_b)
    kept = (k0, k1, k2, k3, k4, k5)
    later = []
    s_count, v_count = [0] * NX, [0] * NX
    for wave in range(NX):
        if wave:
            for group in range(len(GROUPS)):
                for side in range(2):
                    gathered(side, group, wave).wait()
        prepare(wave)
        tiles = []
        for o in list(range(1, wave)) + ([0] if wave else []):
            tiles += [(wave, o), (o, wave)]
        tiles.append((wave, wave))
        places = []
        for n, (a, b) in enumerate(tiles):
            own = (a == 0) != (b == 0)
            places.append(kept[2 * (a + b - 1) + (a == 0)] if own else bufs[n % 2])
        tops = scores(*tiles[0], places[0])
        for n, (a, b) in enumerate(tiles):
            following = None
            if n + 1 < len(tiles):
                following = scores(*tiles[n + 1], places[n + 1])
            if a or not b:
                weigh_sensor(a, b, places[n], tops[1], s_count[a] == 0, s_count[a] == NX - 1)
                s_count[a] += 1
            else:
                later.append((weigh_sensor, a, b, places[n], tops[1]))
            if b or not a:
                weigh_video(a, b, places[n], tops[0], v_count[b] == 0, v_count[b] == NX - 1)
                v_count[b] += 1
            else:
                later.append((weigh_video, a, b, places[n], tops[0]))
            tops = following
    for part, a, b, place, top in later:
        part(a, b, place, top, False, a + b == NX - 1)

    def combine(side):
        for o in (1, 2, 3):
            pltpu.make_async_remote_copy(
                src_ref=num_out.at[side, o], dst_ref=num_in.at[side, o],
                send_sem=n_send.at[side, o], recv_sem=n_recv.at[side, o],
                device_id=peers[side](shift_xy(o)), device_id_type=MESH,
            ).wait()
            pltpu.make_async_remote_copy(
                src_ref=st_out.at[side, o], dst_ref=st_in.at[side, o],
                send_sem=t_send.at[side, o], recv_sem=t_recv.at[side, o],
                device_id=peers[side](shift_xy(o)), device_id_type=MESH,
            ).wait()
        nums = [num_out[side, 0]] + [num_in[side, o] for o in (1, 2, 3)]
        stats = [st_out[side, 0]] + [st_in[side, o] for o in (1, 2, 3)]
        sums = [jnp.concatenate([s[k:k + 1] for k in range(4)], axis=1) for s in stats]
        highs = [jnp.concatenate([s[k:k + 1] for k in range(4, 8)], axis=1) for s in stats]
        top = jnp.maximum(jnp.maximum(highs[0], highs[1]), jnp.maximum(highs[2], highs[3]))
        total = jnp.zeros((1, CHUNK), F32)
        mixed = jnp.zeros((HEAD, CHUNK), F32)
        for o in range(NX):
            fade = jnp.exp2((highs[o] - top) * C2)
            total = total + sums[o] * fade
            mixed = mixed + nums[o].astype(F32) * fade
        attn = mixed * (1.0 / total)
        pair = jnp.concatenate([attn, pltpu.roll(attn, CHUNK - ROWS // 2, 1)], axis=0)
        a_out[side] = pair.T.astype(BF16).reshape(NP, ROWS, LANES)[:, :ROWS // 2]

        def send_back(d, _):
            s = (core + NP - d) % NP
            q = (z + shift_z(s // 2) + HALF) % HALF * 2 + s % 2
            pltpu.make_async_remote_copy(
                src_ref=a_out.at[side, s], dst_ref=a_in.at[side, p],
                send_sem=r_send.at[side, q], recv_sem=r_recv.at[side, p],
                device_id=zc_peer(q), device_id_type=MESH,
            ).start()
            return 0

        lax.fori_loop(1, NP, send_back, 0)
        a_in[side, p] = a_out[side, core]

    def wait_back(side):
        def wait(d, _):
            q = (p + d) % NP
            pltpu.make_async_remote_copy(
                src_ref=a_out.at[side, 0], dst_ref=a_in.at[side, q],
                send_sem=r_send.at[side, q], recv_sem=r_recv.at[side, q],
                device_id=zc_peer(q), device_id_type=MESH,
            ).wait()
            return 0

        lax.fori_loop(1, NP, wait, 0)

    half_low = low[:ROWS // 2]

    def finish(side, gain):
        wait_back(side)
        parts = []
        for k in range(H // 2):
            a = a_in[side, 2 * k].astype(F32)
            b = a_in[side, 2 * k + 1].astype(F32)
            upper = jnp.where(half_low, a, pltpu.roll(b, HEAD, 1))
            lower = jnp.where(half_low, pltpu.roll(a, HEAD, 1), b)
            parts.append(jnp.concatenate([upper, lower], axis=0))
        mixed = jnp.concatenate(parts, axis=1)
        power = jnp.mean(mixed * mixed, axis=-1, keepdims=True)
        normed = (mixed * lax.rsqrt(power + 1e-6) * gain[...]).astype(BF16)
        update = jnp.dot(normed, wbuf[4 + side], preferred_element_type=F32)
        update_out[side * ROWS:(side + 1) * ROWS] = update

    combine(0)
    loads[4].wait()
    loads[5].wait()
    combine(1)
    finish(0, s_gain)
    finish(1, v_gain)


def local(sensor, video, w_sr, w_vr, w_su, w_vu, w_so, w_vo, s_gain, v_gain):
    vmem = pl.BlockSpec(memory_space=pltpu.VMEM)
    hbm = pl.BlockSpec(memory_space=pl.ANY)
    dma = pltpu.SemaphoreType.DMA
    update = pl.pallas_call(
        kernel,
        out_shape=jax.ShapeDtypeStruct((2 * ROWS, D), F32),
        in_specs=[vmem, vmem] + [hbm] * 6 + [vmem, vmem],
        out_specs=vmem,
        scratch_shapes=[
            pltpu.VMEM((6, D, D), BF16),
            pltpu.VMEM((2, NP, ROWS, LANES), BF16),
            pltpu.VMEM((2, NX, NP, ROWS, LANES), BF16),
            pltpu.VMEM((NX, AUG, CHUNK), BF16),
            pltpu.VMEM((2, NX, HEAD, CHUNK), BF16),
            pltpu.VMEM((2, NX, 8, LANES), F32),
            pltpu.VMEM((2, NX, HEAD, CHUNK), BF16),
            pltpu.VMEM((2, NX, 8, LANES), F32),
            pltpu.VMEM((2, NP, ROWS // 2, LANES), BF16),
            pltpu.VMEM((2, NP, ROWS // 2, LANES), BF16),
            pltpu.VMEM((NX, CHUNK, LANES), BF16),
            pltpu.VMEM((NX, CHUNK, LANES), BF16),
            pltpu.VMEM((NX, AUG, CHUNK), F32),
            pltpu.VMEM((NX, 8, CHUNK), F32),
            pltpu.VMEM((NX, CHUNK, LANES), F32),
            pltpu.VMEM((NX, CHUNK, LANES), F32),
            pltpu.VMEM((2, CHUNK, BLK), F32),
            pltpu.VMEM((2, CHUNK, BLK), F32),
            pltpu.VMEM((2, CHUNK, BLK), F32),
            pltpu.VMEM((2, CHUNK, BLK), F32),
            pltpu.VMEM((2, CHUNK, BLK), F32),
            pltpu.VMEM((2, CHUNK, BLK), F32),
            pltpu.VMEM((2, CHUNK, BLK), F32),
            pltpu.VMEM((2, CHUNK, BLK), F32),
            dma((6,)),
            dma((2, NP)), dma((2, NP)),
            dma((2, len(GROUPS), NX)), dma((2, len(GROUPS), NX)),
            dma((2, NX)), dma((2, NX)),
            dma((2, NX)), dma((2, NX)),
            dma((2, NP)), dma((2, NP)),
        ],
        compiler_params=pltpu.CompilerParams(
            collective_id=0, has_side_effects=True, vmem_limit_bytes=60 * 1024 * 1024
        ),
    )(
        sensor, video, w_sr, w_vr, w_su, w_vu, w_so, w_vo,
        s_gain.reshape(1, D), v_gain.reshape(1, D),
    )
    return (
        (sensor.astype(F32) + update[:ROWS]).astype(BF16),
        (video.astype(F32) + update[ROWS:]).astype(BF16),
    )


def solution(mesh):
    rows = P(("blk", "quarter"), None)
    return jax.shard_map(
        local,
        mesh=mesh,
        in_specs=(rows, rows) + (P(),) * 8,
        out_specs=(rows, rows),
        check_vma=False,
    )
```

```python
import functools
import math

import jax
import jax.numpy as jnp
from jax import lax
from jax.experimental import pallas as pl
from jax.experimental.pallas import tpu as pltpu
from jax.sharding import PartitionSpec as P

H = 16
MESH = pl.DeviceIdType.MESH
F32 = jnp.float32
BF16 = jnp.bfloat16
NX = 4
NY = 4
NP = 16
ROWS = 32
D = 1024
LANES = 128
HEAD = 64
CHUNK = NP * ROWS
TOK = NX * CHUNK
NT = (((1,), (1,)), ((), ()))
C2 = math.log2(math.e) * HEAD ** -0.5
AUG = 80
BLK = 256
HALF = NP // 2
GROUPS = ((0, 8), (8, 4), (12, 4))


def shift_z(t):
    return (t % 2) * ((t + 1) // 2) - (1 - t % 2) * (t // 2)


def shift_xy(o):
    return o + o // 2 - 2 * (o // 3)


MIRROR = (0, 2, 1, 3)


def kernel(
    sensor, video, w_sr, w_vr, w_su, w_vu, w_so, w_vo, s_gain, v_gain,
    update_out,
    wbuf, stage, chunks, s_ut, num_out, st_out, num_in, st_in, a_out, a_in, v_ref, v_val, v_acc, v_top, s_acc, s_top, sbuf_a, sbuf_b, k0, k1, k2, k3, k4, k5,
    w_sem, z_send, z_recv, g_send, g_recv, n_send, n_recv, t_send, t_recv, r_send, r_recv,
):
    blk = lax.axis_index("blk")
    quarter = lax.axis_index("quarter")
    core = blk % 2
    x_lo = (blk // 2) % 2
    z = blk // 4
    x_hi = quarter % 2
    y = quarter // 2
    x = x_hi * 2 + x_lo
    p = z * 2 + core

    def zc_peer(q):
        return (((q // 2) * 2 + x_lo) * 2 + q % 2, quarter)

    def x_peer(d):
        k = (x + d) % NX
        return ((z * 2 + k % 2) * 2 + core, y * 2 + k // 2)

    def y_peer(d):
        return (blk, (y + d) % NY * 2 + x_hi)

    peers = (x_peer, y_peer)
    weights = (w_sr, w_su, w_vr, w_vu, w_so, w_vo)
    loads = [pltpu.make_async_copy(w, wbuf.at[k], w_sem.at[k]) for k, w in enumerate(weights)]
    for load in loads:
        load.start()

    barrier = pltpu.get_barrier_semaphore()

    def greet_zc(d, _):
        pl.semaphore_signal(barrier, inc=1, device_id=zc_peer((p + d) % NP), device_id_type=MESH)
        return 0

    def greet_xy(d, _):
        pl.semaphore_signal(barrier, inc=1, device_id=x_peer(d), device_id_type=MESH)
        pl.semaphore_signal(barrier, inc=1, device_id=y_peer(d), device_id_type=MESH)
        return 0

    lax.fori_loop(1, NP, greet_zc, 0)
    lax.fori_loop(1, NX, greet_xy, 0)

    low = lax.broadcasted_iota(jnp.int32, (ROWS, LANES), 1) < HEAD

    def project(rows, first, side):
        loads[first].wait()
        ref = jnp.dot(rows[...], wbuf[first], preferred_element_type=F32)
        loads[first + 1].wait()
        val = jnp.dot(rows[...], wbuf[first + 1], preferred_element_type=F32)
        for k in range(H // 2):
            a = ref[:, k * LANES:(k + 1) * LANES]
            b = val[:, k * LANES:(k + 1) * LANES]
            stage[side, 2 * k] = jnp.where(low, a, pltpu.roll(b, HEAD, 1)).astype(BF16)
            stage[side, 2 * k + 1] = jnp.where(low, pltpu.roll(a, HEAD, 1), b).astype(BF16)

    def head_copy(side, s, sender):
        t = s // 2
        sign = -1 if sender else 1
        there = (z + sign * shift_z(t) + HALF) % HALF
        q = there * 2 + s % 2
        return pltpu.make_async_remote_copy(
            src_ref=stage.at[side, q],
            dst_ref=chunks.at[side, 0, t * 2 + core if sender else s],
            send_sem=z_send.at[side, s],
            recv_sem=z_recv.at[side, t * 2 + core if sender else s],
            device_id=(there * 4 + x_lo * 2 + s % 2, quarter), device_id_type=MESH,
        )

    def send_heads(side, group):
        first, size = GROUPS[group]
        if group == 0:
            head_copy(side, 1 - core, True).start()
        for s in range(2 if group == 0 else first, first + size):
            head_copy(side, s, True).start()
        if group == 0:
            chunks[side, 0, core] = stage[side, p]

    def await_heads(side, group):
        def wait(d, _):
            first, size = GROUPS[group]
            s = (core + d) % size if group == 0 else first + d
            head_copy(side, s, False).wait()
            return 0

        lax.fori_loop(1 if group == 0 else 0, GROUPS[group][1], wait, 0)

    def gather_copy(side, group, o):
        part = pl.ds(*GROUPS[group])
        return pltpu.make_async_remote_copy(
            src_ref=chunks.at[side, 0, part], dst_ref=chunks.at[side, MIRROR[o], part],
            send_sem=g_send.at[side, group, o], recv_sem=g_recv.at[side, group, MIRROR[o]],
            device_id=peers[side](shift_xy(o)), device_id_type=MESH,
        )

    def gathered(side, group, o):
        part = pl.ds(*GROUPS[group])
        return pltpu.make_async_remote_copy(
            src_ref=chunks.at[side, 0, part], dst_ref=chunks.at[side, o, part],
            send_sem=g_send.at[side, group, o], recv_sem=g_recv.at[side, group, o],
            device_id=peers[side](shift_xy(o)), device_id_type=MESH,
        )

    project(sensor, 0, 0)
    project(video, 2, 1)
    pl.semaphore_wait(barrier, (NP - 1) + (NX - 1) + (NY - 1))
    for group in range(len(GROUPS)):
        for side in range(2):
            send_heads(side, group)
    for group in range(len(GROUPS)):
        for side in range(2):
            await_heads(side, group)
            for o in (1, 2):
                gather_copy(side, group, o).start()
    for group in range(len(GROUPS)):
        for side in range(2):
            gather_copy(side, group, 3).start()

    head_rows = lax.broadcasted_iota(jnp.int32, (AUG, LANES), 0) < AUG - HEAD
    pick = (
        lax.broadcasted_iota(jnp.int32, (AUG, LANES), 1)
        == lax.broadcasted_iota(jnp.int32, (AUG, LANES), 0) + (LANES - AUG)
    )
    select = jnp.where(jnp.logical_and(pick, jnp.logical_not(head_rows)), 1.0, 0.0).astype(BF16)
    top_rows = lax.broadcasted_iota(jnp.int32, (AUG, CHUNK), 0) < AUG - HEAD
    keep = lax.broadcasted_iota(jnp.int32, (CHUNK, LANES), 1) < HEAD

    def chunk(side, o):
        return chunks[side, o].reshape(CHUNK, LANES)

    def prepare(o):
        t = lax.dot_general(select, chunk(0, o), NT, preferred_element_type=F32)
        s_ut[o] = jnp.where(top_rows, 1.0, t).astype(BF16)
        v_ref[o] = jnp.where(keep, chunk(1, o), jnp.zeros((), BF16))
        v_val[o] = jnp.where(keep, jnp.ones((), BF16), chunk(1, o))

    halves = [slice(half * BLK, (half + 1) * BLK) for half in range(CHUNK // BLK)]

    def scores(a, b, buf):
        cols, rows = [], None
        for n, part in enumerate(halves):
            s = lax.dot_general(chunk(0, a), v_ref[b, part], NT, preferred_element_type=F32)
            buf[n] = s
            cols.append(jnp.max(s, axis=0, keepdims=True))
            r = jnp.maximum(s[:, :LANES], s[:, LANES:])
            rows = r if rows is None else jnp.maximum(rows, r)
        rows = jnp.broadcast_to(jnp.max(rows, axis=1, keepdims=True), (CHUNK, LANES))
        return cols, rows

    def publish(side, o):
        there = MIRROR[o]
        pltpu.make_async_remote_copy(
            src_ref=num_out.at[side, o], dst_ref=num_in.at[side, there],
            send_sem=n_send.at[side, o], recv_sem=n_recv.at[side, there],
            device_id=peers[side](shift_xy(o)), device_id_type=MESH,
        ).start()
        pltpu.make_async_remote_copy(
            src_ref=st_out.at[side, o], dst_ref=st_in.at[side, there],
            send_sem=t_send.at[side, o], recv_sem=t_recv.at[side, there],
            device_id=peers[side](shift_xy(o)), device_id_type=MESH,
        ).start()

    top_lane = lax.broadcasted_iota(jnp.int32, (CHUNK, LANES), 1) == 1

    def weigh_video(a, b, buf, cols, fresh, last):
        for n, part in enumerate(halves):
            top = cols[n]
            if not fresh:
                old = v_top[b, 0:1, part]
                top = jnp.maximum(top, old)
            w = jnp.exp2((buf[n] - top) * C2).astype(BF16)
            acc = jnp.dot(s_ut[a], w, preferred_element_type=F32)
            if not fresh:
                acc = acc + v_acc[b, :, part] * jnp.exp2((old - top) * C2)
            if last:
                num_out[1, b, :, part] = acc[AUG - HEAD:].astype(BF16)
                for k in range(BLK // LANES):
                    row = n * (BLK // LANES) + k
                    st_out[1, b, row:row + 1] = acc[0:1, k * LANES:(k + 1) * LANES]
                    st_out[1, b, row + 4:row + 5] = top[:, k * LANES:(k + 1) * LANES]
            else:
                v_acc[b, :, part] = acc
                v_top[b, :, part] = jnp.broadcast_to(top, (8, BLK))
        if last and b:
            publish(1, b)

    def weigh_sensor(a, b, buf, top, fresh, last):
        if not fresh:
            old = s_top[a]
            top = jnp.maximum(top, old)
        wide = jnp.concatenate([top] * (BLK // LANES), axis=1)
        acc = None
        for n, part in enumerate(halves):
            w = jnp.exp2((buf[n] - wide) * C2).astype(BF16)
            term = jnp.dot(w, v_val[b, part], preferred_element_type=F32)
            acc = term if acc is None else acc + term
        if not fresh:
            acc = acc + s_acc[a] * jnp.exp2((old - top) * C2)
        if last:
            t = jnp.where(top_lane, top, acc).T
            num_out[0, a] = t[HEAD:].astype(BF16)
            for k in range(CHUNK // LANES):
                st_out[0, a, k:k + 1] = t[0:1, k * LANES:(k + 1) * LANES]
                st_out[0, a, k + 4:k + 5] = t[1:2, k * LANES:(k + 1) * LANES]
            if a:
                publish(0, a)
        else:
            s_acc[a] = acc
            s_top[a] = top

    bufs = (sbuf_a, sbuf_b)
    kept = (k0, k1, k2, k3, k4, k5)
    later = []
    s_count, v_count = [0] * NX, [0] * NX
    for wave in range(NX):
        if wave:
            for group in range(len(GROUPS)):
                for side in range(2):
                    gathered(side, group, wave).wait()
        prepare(wave)
        tiles = []
        for o in list(range(1, wave)) + ([0] if wave else []):
            tiles += [(wave, o), (o, wave)]
        tiles.append((wave, wave))
        places = []
        for n, (a, b) in enumerate(tiles):
            own = (a == 0) != (b == 0)
            places.append(kept[2 * (a + b - 1) + (a == 0)] if own else bufs[n % 2])
        tops = scores(*tiles[0], places[0])
        for n, (a, b) in enumerate(tiles):
            following = None
            if n + 1 < len(tiles):
                following = scores(*tiles[n + 1], places[n + 1])
            if a or not b:
                weigh_sensor(a, b, places[n], tops[1], s_count[a] == 0, s_count[a] == NX - 1)
                s_count[a] += 1
            else:
                later.append((weigh_sensor, a, b, places[n], tops[1]))
            if b or not a:
                weigh_video(a, b, places[n], tops[0], v_count[b] == 0, v_count[b] == NX - 1)
                v_count[b] += 1
            else:
                later.append((weigh_video, a, b, places[n], tops[0]))
            tops = following
    for part, a, b, place, top in later:
        part(a, b, place, top, False, a + b == NX - 1)

    def combine(side):
        for o in (1, 2, 3):
            pltpu.make_async_remote_copy(
                src_ref=num_out.at[side, o], dst_ref=num_in.at[side, o],
                send_sem=n_send.at[side, o], recv_sem=n_recv.at[side, o],
                device_id=peers[side](shift_xy(o)), device_id_type=MESH,
            ).wait()
            pltpu.make_async_remote_copy(
                src_ref=st_out.at[side, o], dst_ref=st_in.at[side, o],
                send_sem=t_send.at[side, o], recv_sem=t_recv.at[side, o],
                device_id=peers[side](shift_xy(o)), device_id_type=MESH,
            ).wait()
        nums = [num_out[side, 0]] + [num_in[side, o] for o in (1, 2, 3)]
        stats = [st_out[side, 0]] + [st_in[side, o] for o in (1, 2, 3)]
        sums = [jnp.concatenate([s[k:k + 1] for k in range(4)], axis=1) for s in stats]
        highs = [jnp.concatenate([s[k:k + 1] for k in range(4, 8)], axis=1) for s in stats]
        top = jnp.maximum(jnp.maximum(highs[0], highs[1]), jnp.maximum(highs[2], highs[3]))
        total = jnp.zeros((1, CHUNK), F32)
        mixed = jnp.zeros((HEAD, CHUNK), F32)
        for o in range(NX):
            fade = jnp.exp2((highs[o] - top) * C2)
            total = total + sums[o] * fade
            mixed = mixed + nums[o].astype(F32) * fade
        attn = mixed * (1.0 / total)
        pair = jnp.concatenate([attn, pltpu.roll(attn, CHUNK - ROWS // 2, 1)], axis=0)
        a_out[:, side] = pair.T.astype(BF16).reshape(NP, ROWS, LANES)[:, :ROWS // 2]

    def send_back(s):
        there = (z + shift_z(s // 2) + HALF) % HALF
        pltpu.make_async_remote_copy(
            src_ref=a_out.at[s], dst_ref=a_in.at[p],
            send_sem=r_send.at[there * 2 + s % 2], recv_sem=r_recv.at[p],
            device_id=(there * 4 + x_lo * 2 + s % 2, quarter), device_id_type=MESH,
        ).start()

    def wait_back():
        def wait(d, _):
            q = (p + d) % NP
            pltpu.make_async_remote_copy(
                src_ref=a_out.at[0], dst_ref=a_in.at[q],
                send_sem=r_send.at[q], recv_sem=r_recv.at[q],
                device_id=zc_peer(q), device_id_type=MESH,
            ).wait()
            return 0

        lax.fori_loop(1, NP, wait, 0)

    half_low = low[:ROWS // 2]

    def finish(side, gain):
        parts = []
        for k in range(H // 2):
            a = a_in[2 * k, side].astype(F32)
            b = a_in[2 * k + 1, side].astype(F32)
            upper = jnp.where(half_low, a, pltpu.roll(b, HEAD, 1))
            lower = jnp.where(half_low, pltpu.roll(a, HEAD, 1), b)
            parts.append(jnp.concatenate([upper, lower], axis=0))
        mixed = jnp.concatenate(parts, axis=1)
        power = jnp.mean(mixed * mixed, axis=-1, keepdims=True)
        normed = (mixed * lax.rsqrt(power + 1e-6) * gain[...]).astype(BF16)
        update = jnp.dot(normed, wbuf[4 + side], preferred_element_type=F32)
        update_out[side * ROWS:(side + 1) * ROWS] = update

    combine(0)
    loads[4].wait()
    loads[5].wait()
    combine(1)
    for s in range(NP - 1, 1, -1):
        send_back(s)
    send_back(1 - core)
    a_in[p] = a_out[core]
    wait_back()
    finish(0, s_gain)
    finish(1, v_gain)


def local(sensor, video, w_sr, w_vr, w_su, w_vu, w_so, w_vo, s_gain, v_gain):
    vmem = pl.BlockSpec(memory_space=pltpu.VMEM)
    hbm = pl.BlockSpec(memory_space=pl.ANY)
    dma = pltpu.SemaphoreType.DMA
    update = pl.pallas_call(
        kernel,
        out_shape=jax.ShapeDtypeStruct((2 * ROWS, D), F32),
        in_specs=[vmem, vmem] + [hbm] * 6 + [vmem, vmem],
        out_specs=vmem,
        scratch_shapes=[
            pltpu.VMEM((6, D, D), BF16),
            pltpu.VMEM((2, NP, ROWS, LANES), BF16),
            pltpu.VMEM((2, NX, NP, ROWS, LANES), BF16),
            pltpu.VMEM((NX, AUG, CHUNK), BF16),
            pltpu.VMEM((2, NX, HEAD, CHUNK), BF16),
            pltpu.VMEM((2, NX, 8, LANES), F32),
            pltpu.VMEM((2, NX, HEAD, CHUNK), BF16),
            pltpu.VMEM((2, NX, 8, LANES), F32),
            pltpu.VMEM((NP, 2, ROWS // 2, LANES), BF16),
            pltpu.VMEM((NP, 2, ROWS // 2, LANES), BF16),
            pltpu.VMEM((NX, CHUNK, LANES), BF16),
            pltpu.VMEM((NX, CHUNK, LANES), BF16),
            pltpu.VMEM((NX, AUG, CHUNK), F32),
            pltpu.VMEM((NX, 8, CHUNK), F32),
            pltpu.VMEM((NX, CHUNK, LANES), F32),
            pltpu.VMEM((NX, CHUNK, LANES), F32),
            pltpu.VMEM((2, CHUNK, BLK), F32),
            pltpu.VMEM((2, CHUNK, BLK), F32),
            pltpu.VMEM((2, CHUNK, BLK), F32),
            pltpu.VMEM((2, CHUNK, BLK), F32),
            pltpu.VMEM((2, CHUNK, BLK), F32),
            pltpu.VMEM((2, CHUNK, BLK), F32),
            pltpu.VMEM((2, CHUNK, BLK), F32),
            pltpu.VMEM((2, CHUNK, BLK), F32),
            dma((6,)),
            dma((2, NP)), dma((2, NP)),
            dma((2, len(GROUPS), NX)), dma((2, len(GROUPS), NX)),
            dma((2, NX)), dma((2, NX)),
            dma((2, NX)), dma((2, NX)),
            dma((NP,)), dma((NP,)),
        ],
        compiler_params=pltpu.CompilerParams(
            collective_id=0, has_side_effects=True, vmem_limit_bytes=60 * 1024 * 1024
        ),
    )(
        sensor, video, w_sr, w_vr, w_su, w_vu, w_so, w_vo,
        s_gain.reshape(1, D), v_gain.reshape(1, D),
    )
    return (
        (sensor.astype(F32) + update[:ROWS]).astype(BF16),
        (video.astype(F32) + update[ROWS:]).astype(BF16),
    )


def solution(mesh):
    rows = P(("blk", "quarter"), None)
    return jax.shard_map(
        local,
        mesh=mesh,
        in_specs=(rows, rows) + (P(),) * 8,
        out_specs=(rows, rows),
        check_vma=False,
    )
```
